512 devices in a mesh: enc: 8 (over x, z_hi), ctx: 8 (over y, core), head: 8 (over z_lo).
Axes of the slice: x: 4, y: 4, z: 16 (z_hi: 2, z_lo: 8; z = z_hi * 8 + z_lo), core: 2. Of those that a mesh axis runs over, the one named last changes fastest.
Arguments:
- text_rows: bfloat16 [65536, 8, 768], P(('enc', 'ctx', 'head')), may hold values from -16 to 16
- vision_rows: bfloat16 [32768, 8, 768], P(('enc', 'ctx'), 'head'), may hold values from -6 to 6
- vision_pos: int32 [32768], replicated, may hold values from 0 to 65535, as said below
- doc_ids: int32 [65536], P(('enc', 'ctx')), may hold values from 0 to 511, never falling along the last dimension, each value on 1 to 256 neighbouring positions
Outputs:
- attended: bfloat16 [65536, 8, 512], P(('enc', 'ctx', 'head'))
The draws below stay inside these ranges and needn't reach their ends.
Inputs may be any that keep to these rules, and one draw needn't show every extreme that they name: `vision_pos`: the positions are distinct. Entries k * 512 to (k + 1) * 512 - 1 are the rows of encoder group k (in the order of enc+ctx) and rise. At most 16 rows of one group lie among the 1024 positions m * 1024 to (m + 1) * 1024 - 1 of one context shard; in every draw some context shard receives exactly 16 rows from every group.
All inputs are finite; a program needn't handle non-finite values.
Results may differ from the reference program's by a relative error of at most 0.0032.
Values may be sent and summed in bfloat16 or wider, within the bound.
No kernel may reach another device: no remote copies, remote signals or barrier semaphores. Data moves between devices by JAX's collectives and lax.ppermute only.
A program may use at most 64 MiB of HBM per device.

```python
import math
import jax
import jax.numpy as jnp
import numpy as np
from jax import lax

HD = 128
KVH = 8
QPG = 4
TOKENS = 65536
R_ROWS = 1024
REACH = 256
SOURCES = 64
SLOTS = 16
V_DEV = 512
VROWS = 32768
DOCS = 512


def draw_text_rows(key, part):
    key = jax.random.fold_in(key, 5)
    base_key = jax.random.fold_in(key, 0)
    full_shape = (TOKENS, KVH, (QPG + 2) * HD)
    entries = jnp.clip(jax.random.normal(base_key, full_shape, jnp.float32), -6.0, 6.0)
    return entries.astype(jnp.bfloat16)


def draw_vision_pos(key, part):
    key = jax.random.fold_in(key, 9)
    swing_key, column_key, offset_key = jax.random.split(key, 3)
    half_cap = SLOTS // 2
    pair_count = SOURCES // 2
    swing = jax.random.randint(swing_key, (SOURCES, pair_count), -half_cap, half_cap + 1)
    chosen = jax.random.randint(column_key, (), 0, pair_count)
    swing = jnp.where(jnp.arange(pair_count)[None, :] == chosen, half_cap, swing)
    loads = half_cap + jnp.stack([swing, -swing], axis=2).reshape(SOURCES, SOURCES)
    arrivals = jnp.sum(loads, axis=0)
    leading = jax.random.randint(offset_key, (SOURCES,), 0, R_ROWS - arrivals + 1)
    before = jnp.cumsum(loads, axis=0) - loads
    base_pos = jnp.arange(SOURCES)[None, :] * R_ROWS + leading[None, :] + before
    through = jnp.cumsum(loads, axis=1)
    prior = through - loads
    row_ids = jnp.arange(V_DEV)
    target = jnp.sum(through[:, None, :] <= row_ids[None, :, None], axis=2)
    within = row_ids[None, :] - jnp.take_along_axis(prior, target, axis=1)
    placed = jnp.take_along_axis(base_pos, target, axis=1) + within
    return placed.reshape(VROWS).astype(jnp.int32)


def level_of(key, shape, pieces, low, high):
    gain = 1.0
    for position, parts in pieces:
        heights = jax.random.uniform(jax.random.fold_in(jax.random.fold_in(key, 6), position), (parts,), jnp.float32, low / len(pieces), high / len(pieces))
        gain = gain * jnp.repeat(jnp.exp(heights), shape[position] // parts).reshape((-1,) + (1,) * (len(shape) - 1 - position))
    return gain


def profile(count, total, bound, slope):
    portions = [(1 << 20) // math.isqrt(rank ** slope) + 1 for rank in range(2, count + 1)]
    spare, counts = total - bound - (count - 1), [1] * (count - 1)
    while spare > 0:
        candidates = [i for i in range(count - 1) if counts[i] < bound]
        whole, remaining = sum([portions[i] for i in candidates]), spare
        for i in candidates:
            extra = min(bound - counts[i], max(1, remaining * portions[i] // whole), spare)
            counts[i] = counts[i] + extra
            spare = spare - extra
    return np.array([bound] + counts)


def uneven_parts(stream_key, amount, total, bound, slope):
    if amount == 2:
        one = jax.random.randint(stream_key, (), max(1, total - bound), min(bound, total - 1) + 1)
        return jnp.stack([one, total - one])
    lengths = jnp.asarray(profile(amount, total, bound, slope), jnp.int32)
    twos = (amount - 1) // 2
    source_of, receiver = lengths[1:1 + 2 * twos:2], lengths[2:2 + 2 * twos:2]
    room = jnp.minimum(source_of - 1, bound - receiver)
    passed = jax.random.randint(jax.random.fold_in(stream_key, 1), (twos,), 0, 1 << 20) % (room + 1)
    lengths = lengths.at[1:1 + 2 * twos:2].set(source_of - passed).at[2:2 + 2 * twos:2].set(receiver + passed)
    return lengths[jax.random.permutation(jax.random.fold_in(stream_key, 2), amount)]


def noise(stream_key, dims, deviation, reach, shards=(), held_as=jnp.bfloat16):
    loudness = level_of(stream_key, dims, shards, -0.22, 0.18) if shards else 1.0
    array = jax.random.normal(stream_key, dims, jnp.float32) * deviation * loudness
    return jnp.minimum(jnp.maximum(array, -reach), reach).astype(held_as)


def setup_inputs(seed: int = 0) -> dict:
    streams_of = jax.random.split(jax.random.key(seed), 5)
    return {
        "text_rows": draw_text_rows(jax.random.fold_in(streams_of[4], 71), 0),
        "vision_rows": noise(streams_of[1], (VROWS, KVH, (QPG + 2) * HD), 1.0, 6.0, ((0, 64), (1, 8))),
        "vision_pos": draw_vision_pos(jax.random.fold_in(streams_of[4], 71), 0),
        "doc_ids": jnp.searchsorted(jnp.cumsum(uneven_parts(streams_of[3], DOCS, TOKENS, REACH, 2)), jnp.arange(TOKENS), side="right").astype(jnp.int32),
    }


def attend_block(queries, key_rows, value_rows, query_docs, key_docs, offset, factor):
    scores = jnp.einsum("qghd,kgd->ghqk", queries.astype(jnp.float32), key_rows.astype(jnp.float32)) * factor
    query_pos = offset + jnp.arange(queries.shape[0], dtype=jnp.int32)
    key_pos = jnp.arange(key_rows.shape[0], dtype=jnp.int32)
    allowed = (key_docs[None, :] == query_docs[:, None]) & (key_pos[None, :] <= query_pos[:, None])
    masked = jnp.where(allowed, scores, -jnp.inf)
    row_max = jnp.max(masked, axis=-1, keepdims=True)
    expo_terms = jnp.where(allowed, jnp.exp(masked - row_max), 0.0)
    row_total = jnp.sum(expo_terms, axis=-1)
    weights = expo_terms.astype(jnp.bfloat16)
    summed = jnp.einsum("ghqk,kgd->qghd", weights.astype(jnp.float32), value_rows.astype(jnp.float32))
    return summed / jnp.transpose(row_total, (2, 0, 1))[..., None]


def reference(text_rows, vision_rows, vision_pos, doc_ids):
    merged = text_rows.at[vision_pos].set(vision_rows)
    block_rows = R_ROWS // 2
    query_width = QPG * HD
    padded = jnp.concatenate([jnp.zeros((REACH, KVH, (QPG + 2) * HD), merged.dtype), merged], 0)
    padded_docs = jnp.concatenate([jnp.full((REACH,), -1, jnp.int32), doc_ids.astype(jnp.int32)], 0)
    factor = HD ** -0.5

    def one_block(block_index):
        first_row = (block_index * block_rows).astype(jnp.int32)
        queries = lax.dynamic_slice_in_dim(merged, first_row, block_rows, 0)[:, :, :query_width]
        queries = queries.reshape(block_rows, KVH, QPG, HD)
        query_docs = lax.dynamic_slice_in_dim(doc_ids, first_row, block_rows, 0)
        window = lax.dynamic_slice_in_dim(padded, first_row, REACH + block_rows, 0)
        window_docs = lax.dynamic_slice_in_dim(padded_docs, first_row, REACH + block_rows, 0)
        attended = attend_block(queries, window[:, :, query_width:query_width + HD], window[:, :, query_width + HD:], query_docs, window_docs, REACH, factor)
        return attended.reshape(block_rows, KVH, query_width).astype(jnp.bfloat16)

    blocks = lax.map(one_block, jnp.arange(TOKENS // block_rows, dtype=jnp.int32))
    return blocks.reshape(TOKENS, KVH, query_width)
```

```python
import functools

import jax
import jax.numpy as jnp
from jax import lax
from jax.experimental import pallas as pl
from jax.experimental.pallas import tpu as pltpu
from jax.sharding import Mesh
from jax.sharding import PartitionSpec as P

HD = 128
QPG = 4
GROUPS = 8
QW = QPG * HD
KW = 2 * HD
ROWS = 128
SHARD = 1024
SLOTS = 16
PER_SOURCE = 512
REACH = 256
AXES = ("x", "zh", "y", "c", "zl")
SIZES = (4, 2, 4, 2, 8)
COUNT = 512
VMEM = 48 * 1024 * 1024


def flat_id(x, zh, y, c, zl):
    return (((x * 2 + zh) * 4 + y) * 2 + c) * 8 + zl


def pairs(move):
    ids = []
    for x in range(4):
        for zh in range(2):
            for y in range(4):
                for c in range(2):
                    for zl in range(8):
                        ids.append((flat_id(x, zh, y, c, zl), flat_id(*move(x, zh, y, c, zl))))
    return ids


def to_other_half(value):
    return lax.ppermute(value, AXES, pairs(lambda x, zh, y, c, zl: (x, 1 - zh, y, c, zl)))


def along_head(value, steps):
    return lax.ppermute(value, AXES, pairs(lambda x, zh, y, c, zl: (x, zh, y, c, (zl + steps) % 8)))


def from_behind(value, steps):
    return lax.ppermute(value, AXES, [(i, i + steps) for i in range(COUNT - steps)])


def over_columns(slots):
    width = slots.shape[-1]
    swapped = lax.all_to_all(
        slots.reshape(32, SLOTS, width), ("x", "y", "c"), split_axis=0, concat_axis=0, tiled=True
    )
    return swapped.reshape(32 * SLOTS, width)


def onehot_rows(first, codes):
    rows = lax.broadcasted_iota(jnp.int32, (ROWS, codes.shape[1]), 0) + first
    return jnp.where(rows == codes, 1.0, 0.0).astype(jnp.bfloat16)


def slots_kernel(code_ref, rows_ref, out_ref):
    for part in range(PER_SOURCE // ROWS):
        pick = onehot_rows(part * ROWS, code_ref[...])
        placed = jnp.dot(pick, rows_ref[...], preferred_element_type=jnp.float32)
        out_ref[part * ROWS : (part + 1) * ROWS, :] = placed.astype(jnp.bfloat16)


def vmem():
    return pl.BlockSpec(memory_space=pltpu.VMEM)


def smem():
    return pl.BlockSpec(memory_space=pltpu.SMEM)


def params():
    return pltpu.CompilerParams(vmem_limit_bytes=VMEM)


def to_slots(code, rows):
    return pl.pallas_call(
        slots_kernel,
        out_shape=jax.ShapeDtypeStruct((PER_SOURCE, rows.shape[1]), jnp.bfloat16),
        in_specs=[vmem(), vmem()],
        out_specs=vmem(),
        compiler_params=params(),
        name="to_slots",
    )(code, rows)


def blocks_kernel(low, high, zl_ref, near_code, far_code, near_ref, far_ref, *outs):
    zl = zl_ref[0]
    for step in range(GROUPS):
        first = lax.rem(zl + step, GROUPS) * ROWS
        near = jnp.dot(
            onehot_rows(first, near_code[...]),
            near_ref[:, low:high],
            preferred_element_type=jnp.float32,
        )
        far = jnp.dot(
            onehot_rows(first, far_code[...]), far_ref[...], preferred_element_type=jnp.float32
        )
        outs[step][...] = (near + far).astype(jnp.bfloat16)


def to_blocks(zl, near_code, far_code, near, far, low, high):
    shape = jax.ShapeDtypeStruct((ROWS, high - low), jnp.bfloat16)
    return pl.pallas_call(
        functools.partial(blocks_kernel, low, high),
        out_shape=[shape] * GROUPS,
        in_specs=[smem()] + [vmem()] * 4,
        out_specs=[vmem()] * GROUPS,
        compiler_params=params(),
        name="to_blocks",
    )(zl, near_code, far_code, near, far)


def landed(first, landing):
    rows = lax.broadcasted_iota(jnp.int32, (ROWS, landing.shape[1]), 0) + first
    hits = jnp.where(rows == landing, 1.0, 0.0)
    return jnp.max(hits, axis=1, keepdims=True) > 0.0


def merge_kernel(zl_ref, landing_ref, text_ref, *refs):
    arrived, out_ref = refs[:GROUPS], refs[GROUPS]
    zl = zl_ref[0]
    present = landed(zl * ROWS, landing_ref[...])
    for step in range(GROUPS):
        group = lax.rem(zl - step + GROUPS, GROUPS)
        out_ref[group] = jnp.where(present, arrived[step][...], text_ref[group, :, QW:])


def merge_keys(zl, landing, text, arrived):
    return pl.pallas_call(
        merge_kernel,
        out_shape=jax.ShapeDtypeStruct((GROUPS, ROWS, KW), jnp.bfloat16),
        in_specs=[smem()] + [vmem()] * (2 + GROUPS),
        out_specs=vmem(),
        compiler_params=params(),
        name="merge_keys",
    )(zl, landing, text, *arrived)


def attend_kernel(zl_ref, landing_ref, qdoc_ref, kdoc_ref, text_ref, two_ref, one_ref, own_ref, *refs):
    arrived, out_ref = refs[:GROUPS], refs[GROUPS]
    zl = zl_ref[0]
    present = landed(zl * ROWS, landing_ref[...])
    window = REACH + ROWS
    query_pos = lax.broadcasted_iota(jnp.int32, (ROWS, window), 0) + REACH
    key_pos = lax.broadcasted_iota(jnp.int32, (ROWS, window), 1)
    allowed = (kdoc_ref[...] == qdoc_ref[...]) & (key_pos <= query_pos)
    factor = HD ** (-0.5)
    for step in range(GROUPS):
        group = lax.rem(zl - step + GROUPS, GROUPS)
        queries = jnp.where(present, arrived[step][...], text_ref[group, :, :QW])
        joined = jnp.concatenate([two_ref[group], one_ref[group], own_ref[group]], 0)
        keys, values = joined[:, :HD], joined[:, HD:]
        for head in range(QPG):
            cols = slice(head * HD, (head + 1) * HD)
            scores = lax.dot_general(
                queries[:, cols], keys, (((1,), (1,)), ((), ())), preferred_element_type=jnp.float32
            )
            masked = jnp.where(allowed, scores * factor, -jnp.inf)
            row_max = jnp.max(masked, axis=1, keepdims=True)
            terms = jnp.exp(masked - row_max)
            total = jnp.sum(terms, axis=1, keepdims=True)
            summed = jnp.dot(terms.astype(jnp.bfloat16), values, preferred_element_type=jnp.float32)
            out_ref[group, :, cols] = (summed / total).astype(jnp.bfloat16)


def attend(zl, landing, qdoc, kdoc, text, two, one, own, arrived):
    return pl.pallas_call(
        attend_kernel,
        out_shape=jax.ShapeDtypeStruct((GROUPS, ROWS, QW), jnp.bfloat16),
        in_specs=[smem()] + [vmem()] * (7 + GROUPS),
        out_specs=vmem(),
        compiler_params=params(),
        name="attend",
    )(zl, landing, qdoc, kdoc, text, two, one, own, *arrived)


def after(value, *others):
    return lax.optimization_barrier((value, *others))[0]


def body(text_rows, vision_rows, vision_pos, doc_ids):
    rows = vision_rows.reshape(PER_SOURCE, QW + KW)
    half = lax.axis_index("zh")
    zl = lax.axis_index("zl")
    shard = lax.axis_index(("x", "zh", "y", "c"))

    far_kv_rows = to_other_half(rows[:, QW:])

    marks = doc_ids + 1
    prior_marks = from_behind(marks[SHARD - REACH :], 8)

    pos = vision_pos.reshape(64, PER_SOURCE)
    target = pos // SHARD
    index = jnp.arange(PER_SOURCE, dtype=jnp.int32)

    def slot_code(source):
        own = lax.dynamic_index_in_dim(target, source, 0, keepdims=False)
        same = (own[None, :] == own[:, None]) & (index[:, None] < index[None, :])
        rank = jnp.sum(same.astype(jnp.int32), axis=0)
        column = (own // 16) * 8 + own % 8
        code = jnp.where((own // 8) % 2 == half, column * SLOTS + rank, -1)
        return code.reshape(1, PER_SOURCE)

    hit = target == shard
    skip = jnp.sum((target < shard).astype(jnp.int32), axis=1, keepdims=True)
    rank = jnp.where(hit, index[None, :] - skip, -1)
    slot = jnp.arange(SLOTS, dtype=jnp.int32)
    chosen = rank[:, None, :] == slot[None, :, None]
    local = pos - shard * SHARD + 1
    landing = jnp.sum(jnp.where(chosen, local[:, None, :], 0), axis=2) - 1
    landing = landing.reshape(4, 2, 8 * SLOTS)
    near_code = lax.dynamic_index_in_dim(landing, half, 1, keepdims=False).reshape(1, -1)
    far_code = lax.dynamic_index_in_dim(landing, 1 - half, 1, keepdims=False).reshape(1, -1)
    both = jnp.concatenate([near_code, far_code], 1)

    near_out = to_slots(slot_code(shard), rows)
    near = over_columns(near_out)
    far_slot_code = slot_code(shard ^ 8)

    text = jnp.transpose(text_rows, (1, 0, 2))
    joined_marks = jnp.concatenate([prior_marks, marks], 0)
    kdoc = lax.dynamic_slice_in_dim(joined_marks, zl * ROWS, REACH + ROWS).reshape(1, -1)
    qdoc = lax.dynamic_slice_in_dim(marks, zl * ROWS, ROWS).reshape(-1, 1)
    zl_arr = zl.reshape(1)

    far_q_rows = to_other_half(after(rows[:, :QW], far_kv_rows))

    far_kv = over_columns(to_slots(far_slot_code, far_kv_rows))
    kv_blocks = to_blocks(zl_arr, near_code, far_code, near, far_kv, QW, QW + KW)
    order = (4, 3, 5, 2, 6, 1, 7)
    kv_arrived = [kv_blocks[0]] + [None] * 7
    for step in order:
        kv_arrived[step] = along_head(kv_blocks[step], step)

    far_q = over_columns(to_slots(far_slot_code, far_q_rows))
    own_kv = merge_keys(zl_arr, both, text, kv_arrived)
    one_kv = from_behind(own_kv, 1)

    q_blocks = to_blocks(zl_arr, near_code, far_code, near, far_q, 0, QW)
    q_arrived = [q_blocks[0]] + [None] * 7
    for step in order:
        q_arrived[step] = along_head(q_blocks[step], step)
    two_kv = from_behind(one_kv, 1)

    out = attend(zl_arr, both, qdoc, kdoc, text, two_kv, one_kv, own_kv, q_arrived)
    return jnp.transpose(out, (1, 0, 2))


def solution(mesh):
    fine = Mesh(mesh.devices.reshape(SIZES), AXES)
    in_specs = (
        P(AXES, None, None),
        P(("x", "zh", "y", "c"), "zl", None),
        P(),
        P(("x", "zh", "y", "c")),
    )
    return jax.shard_map(
        body, mesh=fine, in_specs=in_specs, out_specs=P(AXES, None, None), check_vma=False
    )
```

```python
import functools

import jax
import jax.numpy as jnp
from jax import lax
from jax.experimental import pallas as pl
from jax.experimental.pallas import tpu as pltpu
from jax.sharding import Mesh
from jax.sharding import PartitionSpec as P

HD = 128
QPG = 4
GROUPS = 8
QW = QPG * HD
KW = 2 * HD
ROWS = 128
SHARD = 1024
SLOTS = 16
PER_SOURCE = 512
REACH = 256
AXES = ("x", "zh", "y", "c", "zl")
SIZES = (4, 2, 4, 2, 8)
COUNT = 512
VMEM = 48 * 1024 * 1024


def flat_id(x, zh, y, c, zl):
    return (((x * 2 + zh) * 4 + y) * 2 + c) * 8 + zl


def pairs(move):
    ids = []
    for x in range(4):
        for zh in range(2):
            for y in range(4):
                for c in range(2):
                    for zl in range(8):
                        ids.append((flat_id(x, zh, y, c, zl), flat_id(*move(x, zh, y, c, zl))))
    return ids


def to_other_half(value):
    return lax.ppermute(value, AXES, pairs(lambda x, zh, y, c, zl: (x, 1 - zh, y, c, zl)))


def along_head(value, steps):
    return lax.ppermute(value, AXES, pairs(lambda x, zh, y, c, zl: (x, zh, y, c, (zl + steps) % 8)))


def from_behind(value, steps):
    return lax.ppermute(value, AXES, [(i, i + steps) for i in range(COUNT - steps)])


def over_columns(slots):
    width = slots.shape[-1]
    swapped = lax.all_to_all(
        slots.reshape(32, SLOTS, width), ("x", "y", "c"), split_axis=0, concat_axis=0, tiled=True
    )
    return swapped.reshape(32 * SLOTS, width)


def onehot_rows(first, codes):
    rows = lax.broadcasted_iota(jnp.int32, (ROWS, codes.shape[1]), 0) + first
    return jnp.where(rows == codes, 1.0, 0.0).astype(jnp.bfloat16)


def slots_kernel(code_ref, rows_ref, out_ref):
    for part in range(PER_SOURCE // ROWS):
        pick = onehot_rows(part * ROWS, code_ref[...])
        placed = jnp.dot(pick, rows_ref[...], preferred_element_type=jnp.float32)
        out_ref[part * ROWS : (part + 1) * ROWS, :] = placed.astype(jnp.bfloat16)


def vmem():
    return pl.BlockSpec(memory_space=pltpu.VMEM)


def smem():
    return pl.BlockSpec(memory_space=pltpu.SMEM)


def params():
    return pltpu.CompilerParams(vmem_limit_bytes=VMEM)


def to_slots(code, rows):
    return pl.pallas_call(
        slots_kernel,
        out_shape=jax.ShapeDtypeStruct((PER_SOURCE, rows.shape[1]), jnp.bfloat16),
        in_specs=[vmem(), vmem()],
        out_specs=vmem(),
        compiler_params=params(),
        name="to_slots",
    )(code, rows)


def blocks_kernel(low, high, zl_ref, near_code, far_code, near_ref, far_ref, *outs):
    zl = zl_ref[0]
    for step in range(GROUPS):
        first = lax.rem(zl + step, GROUPS) * ROWS
        near = jnp.dot(
            onehot_rows(first, near_code[...]),
            near_ref[:, low:high],
            preferred_element_type=jnp.float32,
        )
        far = jnp.dot(
            onehot_rows(first, far_code[...]), far_ref[...], preferred_element_type=jnp.float32
        )
        outs[step][...] = (near + far).astype(jnp.bfloat16)


def to_blocks(zl, near_code, far_code, near, far, low, high):
    shape = jax.ShapeDtypeStruct((ROWS, high - low), jnp.bfloat16)
    return pl.pallas_call(
        functools.partial(blocks_kernel, low, high),
        out_shape=[shape] * GROUPS,
        in_specs=[smem()] + [vmem()] * 4,
        out_specs=[vmem()] * GROUPS,
        compiler_params=params(),
        name="to_blocks",
    )(zl, near_code, far_code, near, far)


def landed(first, landing):
    rows = lax.broadcasted_iota(jnp.int32, (ROWS, landing.shape[1]), 0) + first
    hits = jnp.where(rows == landing, 1.0, 0.0)
    return jnp.max(hits, axis=1, keepdims=True) > 0.0


def merge_kernel(zl_ref, landing_ref, text_ref, *refs):
    arrived, out_ref = refs[:GROUPS], refs[GROUPS]
    zl = zl_ref[0]
    present = landed(zl * ROWS, landing_ref[...])
    for step in range(GROUPS):
        group = lax.rem(zl - step + GROUPS, GROUPS)
        out_ref[group] = jnp.where(present, arrived[step][...], text_ref[group, :, QW:])


def merge_keys(zl, landing, text, arrived):
    return pl.pallas_call(
        merge_kernel,
        out_shape=jax.ShapeDtypeStruct((GROUPS, ROWS, KW), jnp.bfloat16),
        in_specs=[smem()] + [vmem()] * (2 + GROUPS),
        out_specs=vmem(),
        compiler_params=params(),
        name="merge_keys",
    )(zl, landing, text, *arrived)


def attend_kernel(steps, first_steps, zl_ref, landing_ref, qdoc_ref, kdoc_ref, text_ref, two_ref, one_ref, own_ref, *refs):
    arrived, earlier, out_ref = refs[: len(steps)], refs[len(steps) : -1], refs[-1]
    zl = zl_ref[0]
    present = landed(zl * ROWS, landing_ref[...])
    window = REACH + ROWS
    query_pos = lax.broadcasted_iota(jnp.int32, (ROWS, window), 0) + REACH
    key_pos = lax.broadcasted_iota(jnp.int32, (ROWS, window), 1)
    allowed = (kdoc_ref[...] == qdoc_ref[...]) & (key_pos <= query_pos)
    factor = HD ** (-0.5)
    for place, step in enumerate(first_steps):
        out_ref[lax.rem(zl - step + GROUPS, GROUPS)] = earlier[0][place]
    for place, step in enumerate(steps):
        group = lax.rem(zl - step + GROUPS, GROUPS)
        queries = jnp.where(present, arrived[place][...], text_ref[group, :, :QW])
        joined = jnp.concatenate([two_ref[group], one_ref[group], own_ref[group]], 0)
        keys, values = joined[:, :HD], joined[:, HD:]
        row = group if first_steps else place
        for head in range(QPG):
            cols = slice(head * HD, (head + 1) * HD)
            scores = lax.dot_general(
                queries[:, cols], keys, (((1,), (1,)), ((), ())), preferred_element_type=jnp.float32
            )
            masked = jnp.where(allowed, scores * factor, -jnp.inf)
            row_max = jnp.max(masked, axis=1, keepdims=True)
            terms = jnp.exp(masked - row_max)
            total = jnp.sum(terms, axis=1, keepdims=True)
            summed = jnp.dot(terms.astype(jnp.bfloat16), values, preferred_element_type=jnp.float32)
            out_ref[row, :, cols] = (summed / total).astype(jnp.bfloat16)


def attend(steps, first_steps, common, arrived, earlier):
    count = GROUPS if first_steps else len(steps)
    return pl.pallas_call(
        functools.partial(attend_kernel, steps, first_steps),
        out_shape=jax.ShapeDtypeStruct((count, ROWS, QW), jnp.bfloat16),
        in_specs=[smem()] + [vmem()] * (7 + len(steps) + len(earlier)),
        out_specs=vmem(),
        compiler_params=params(),
        name="attend",
    )(*common, *[arrived[step] for step in steps], *earlier)


def body(text_rows, vision_rows, vision_pos, doc_ids):
    rows = vision_rows.reshape(PER_SOURCE, QW + KW)
    half = lax.axis_index("zh")
    zl = lax.axis_index("zl")
    shard = lax.axis_index(("x", "zh", "y", "c"))

    far_kv_rows = to_other_half(rows[:, QW:])
    far_q_rows = to_other_half(rows[:, :QW])

    marks = doc_ids + 1
    prior_marks = from_behind(marks[SHARD - REACH :], 8)

    pos = vision_pos.reshape(64, PER_SOURCE)
    target = pos // SHARD
    index = jnp.arange(PER_SOURCE, dtype=jnp.int32)

    def slot_code(source):
        own = lax.dynamic_index_in_dim(target, source, 0, keepdims=False)
        same = (own[None, :] == own[:, None]) & (index[:, None] < index[None, :])
        rank = jnp.sum(same.astype(jnp.int32), axis=0)
        column = (own // 16) * 8 + own % 8
        code = jnp.where((own // 8) % 2 == half, column * SLOTS + rank, -1)
        return code.reshape(1, PER_SOURCE)

    hit = target == shard
    skip = jnp.sum((target < shard).astype(jnp.int32), axis=1, keepdims=True)
    rank = jnp.where(hit, index[None, :] - skip, -1)
    slot = jnp.arange(SLOTS, dtype=jnp.int32)
    chosen = rank[:, None, :] == slot[None, :, None]
    local = pos - shard * SHARD + 1
    landing = jnp.sum(jnp.where(chosen, local[:, None, :], 0), axis=2) - 1
    landing = landing.reshape(4, 2, 8 * SLOTS)
    near_code = lax.dynamic_index_in_dim(landing, half, 1, keepdims=False).reshape(1, -1)
    far_code = lax.dynamic_index_in_dim(landing, 1 - half, 1, keepdims=False).reshape(1, -1)
    both = jnp.concatenate([near_code, far_code], 1)

    near_out = to_slots(slot_code(shard), rows)
    near = over_columns(near_out)
    far_slot_code = slot_code(shard ^ 8)

    text = jnp.transpose(text_rows, (1, 0, 2))
    joined_marks = jnp.concatenate([prior_marks, marks], 0)
    kdoc = lax.dynamic_slice_in_dim(joined_marks, zl * ROWS, REACH + ROWS).reshape(1, -1)
    qdoc = lax.dynamic_slice_in_dim(marks, zl * ROWS, ROWS).reshape(-1, 1)
    zl_arr = zl.reshape(1)

    far_kv = over_columns(to_slots(far_slot_code, far_kv_rows))
    kv_blocks = to_blocks(zl_arr, near_code, far_code, near, far_kv, QW, QW + KW)
    order = (4, 3, 5, 2, 6, 1, 7)
    kv_arrived = [kv_blocks[0]] + [None] * 7
    for step in order:
        kv_arrived[step] = along_head(kv_blocks[step], step)

    far_q = over_columns(to_slots(far_slot_code, far_q_rows))
    own_kv = merge_keys(zl_arr, both, text, kv_arrived)
    one_kv = from_behind(own_kv, 1)

    q_blocks = to_blocks(zl_arr, near_code, far_code, near, far_q, 0, QW)
    q_arrived = [q_blocks[0]] + [None] * 7
    for step in order:
        q_arrived[step] = along_head(q_blocks[step], step)
    two_kv = from_behind(one_kv, 1)

    common = (zl_arr, both, qdoc, kdoc, text, two_kv, one_kv, own_kv)
    first_steps, last_steps = (0, 4, 3, 5), (2, 6, 1, 7)
    first = attend(first_steps, (), common, q_arrived, ())
    out = attend(last_steps, first_steps, common, q_arrived, (first,))
    return jnp.transpose(out, (1, 0, 2))


def solution(mesh):
    fine = Mesh(mesh.devices.reshape(SIZES), AXES)
    in_specs = (
        P(AXES, None, None),
        P(("x", "zh", "y", "c"), "zl", None),
        P(),
        P(("x", "zh", "y", "c")),
    )
    return jax.shard_map(
        body, mesh=fine, in_specs=in_specs, out_specs=P(AXES, None, None), check_vma=False
    )
```

```python
import functools

import jax
import jax.numpy as jnp
import numpy as np
from jax import lax
from jax.experimental import pallas as pl
from jax.experimental.pallas import tpu as pltpu
from jax.sharding import Mesh
from jax.sharding import PartitionSpec as P

HD = 128
QPG = 4
GROUPS = 8
QW = QPG * HD
KW = 2 * HD
PART = 2 * HD
ROWS = 128
SHARD = 1024
SLOTS = 16
SOURCES = 64
PER_SOURCE = 512
COLUMNS = 32
PLANES = 16
REACH = 256
AXES = ("x", "zh", "y", "c", "zl")
SIZES = (4, 2, 4, 2, 8)
COUNT = 512
VMEM = 48 * 1024 * 1024
PLANE_OF = (15, 1, 3, 10, 14, 9, 2, 5, 13, 7, 8, 4, 0, 11, 6, 12)
UNIT_OF = tuple(int(u) for u in np.argsort(np.array(PLANE_OF)))


def flat_id(x, zh, y, c, zl):
    return (((x * 2 + zh) * 4 + y) * 2 + c) * 8 + zl


def to_plane(value, swapped):
    ids = []
    for x in range(4):
        for y in range(4):
            for c in range(2):
                for zh in range(2):
                    for zl in range(8):
                        plane = PLANE_OF[zl * 2 + (zh ^ swapped)]
                        target = flat_id(x, plane // 8, y, c, plane % 8)
                        ids.append((flat_id(x, zh, y, c, zl), target))
    return lax.ppermute(value, AXES, ids)


def from_behind(value, steps):
    return lax.ppermute(value, AXES, [(i, i + steps) for i in range(COUNT - steps)])


def over_columns(slots):
    return lax.all_to_all(slots, ("x", "y", "c"), split_axis=0, concat_axis=0, tiled=True)


def over_planes(blocks):
    return lax.all_to_all(blocks, ("zh", "zl"), split_axis=0, concat_axis=0, tiled=True)


def after(value, *others):
    return lax.optimization_barrier((value, *others))[0]


def vmem():
    return pl.BlockSpec(memory_space=pltpu.VMEM)


def smem():
    return pl.BlockSpec(memory_space=pltpu.SMEM)


def call(kernel, name, out_shape, scalars, *arrays):
    return pl.pallas_call(
        kernel,
        out_shape=out_shape,
        in_specs=[smem()] * len(scalars) + [vmem()] * len(arrays),
        out_specs=vmem(),
        compiler_params=pltpu.CompilerParams(vmem_limit_bytes=VMEM),
        name=name,
    )(*scalars, *arrays)


def bf16(*shape):
    return jax.ShapeDtypeStruct(shape, jnp.bfloat16)


def pick(first, codes, rows):
    wanted = lax.broadcasted_iota(jnp.int32, (ROWS, codes.shape[1]), 0) + first
    onehot = jnp.where(wanted == codes, 1.0, 0.0).astype(jnp.bfloat16)
    return jnp.dot(onehot, rows, preferred_element_type=jnp.float32).astype(jnp.bfloat16)


def slots_kernel(count, *refs):
    codes, sources, out_ref = refs[:count], refs[count : 2 * count], refs[-1]
    for turn in range(count):
        for part in range(SOURCES * SLOTS // ROWS):
            picked = pick(part * ROWS, codes[turn][...], sources[turn][...])
            for i in range(ROWS // SLOTS):
                column, half = (part * (ROWS // SLOTS) + i) // 2, i % 2
                low = (half * count + turn) * SLOTS
                out_ref[column, low : low + SLOTS, :] = picked[i * SLOTS : (i + 1) * SLOTS]


def to_slots(codes, sources):
    count = len(codes)
    shape = bf16(COLUMNS, 2 * count * SLOTS, sources[0].shape[1])
    return call(functools.partial(slots_kernel, count), "to_slots", shape, (), *codes, *sources)


def blocks_kernel(low_land, high_land, slots_ref, out_ref):
    per_half, width = slots_ref.shape[1] // 2, slots_ref.shape[2]
    for half, landing in enumerate((low_land, high_land)):
        slots = slots_ref[:, half * per_half : (half + 1) * per_half, :]
        slots = slots.reshape(COLUMNS * per_half, width)
        for block in range(GROUPS):
            out_ref[half * GROUPS + block] = pick(block * ROWS, landing[...], slots)


def to_blocks(landings, slots):
    return call(blocks_kernel, "to_blocks", bf16(PLANES, ROWS, slots.shape[2]), (), *landings, slots)


def landed(first, landing):
    rows = lax.broadcasted_iota(jnp.int32, (ROWS, landing.shape[1]), 0) + first
    return jnp.max(jnp.where(rows == landing, 1.0, 0.0), axis=1, keepdims=True) > 0.0


def merge_kernel(zl_ref, landing_ref, text_ref, arrived_ref, out_ref):
    present = landed(zl_ref[0] * ROWS, landing_ref[...])
    for group in range(GROUPS):
        arrived = arrived_ref[group] + arrived_ref[GROUPS + group]
        out_ref[group] = jnp.where(present, arrived, text_ref[group, :, QW:])


def merge_keys(zl, landing, text, arrived):
    return call(merge_kernel, "merge_keys", bf16(GROUPS, ROWS, KW), (zl,), landing, text, arrived)


def attend_kernel(zl_ref, landing_ref, qdoc_ref, kdoc_ref, text_ref, two_ref, one_ref, own_ref, arrived_ref, out_ref):
    present = landed(zl_ref[0] * ROWS, landing_ref[...])
    window = REACH + ROWS
    query_pos = lax.broadcasted_iota(jnp.int32, (ROWS, window), 0) + REACH
    key_pos = lax.broadcasted_iota(jnp.int32, (ROWS, window), 1)
    allowed = (kdoc_ref[...] == qdoc_ref[...]) & (key_pos <= query_pos)
    factor = HD ** (-0.5)
    for group in range(GROUPS):
        joined = jnp.concatenate([two_ref[group], one_ref[group], own_ref[group]], 0)
        keys, values = joined[:, :HD], joined[:, HD:]
        queries = []
        for head in range(QPG):
            low = (head % 2) * HD
            arrived = arrived_ref[PLANE_OF[group * 2 + head // 2], :, low : low + HD]
            text = text_ref[group, :, head * HD : (head + 1) * HD]
            queries.append(jnp.where(present, arrived, text))
        scores = lax.dot_general(
            jnp.concatenate(queries, 0),
            keys,
            (((1,), (1,)), ((), ())),
            preferred_element_type=jnp.float32,
        )
        for head in range(QPG):
            masked = jnp.where(allowed, scores[head * ROWS : (head + 1) * ROWS] * factor, -jnp.inf)
            row_max = jnp.max(masked, axis=1, keepdims=True)
            terms = jnp.exp(masked - row_max)
            total = jnp.sum(terms, axis=1, keepdims=True)
            summed = jnp.dot(terms.astype(jnp.bfloat16), values, preferred_element_type=jnp.float32)
            out_ref[group, :, head * HD : (head + 1) * HD] = (summed / total).astype(jnp.bfloat16)


def body(text_rows, vision_rows, vision_pos, doc_ids):
    rows = vision_rows.reshape(PER_SOURCE, QW + KW)
    x, half, y, c, zl = [lax.axis_index(axis) for axis in AXES]
    zl_arr = zl.reshape(1)
    part = jnp.asarray(UNIT_OF, jnp.int32)[half * 8 + zl] % 2
    text = jnp.transpose(text_rows, (1, 0, 2))

    zero, one = rows[:, :PART], rows[:, PART:QW]
    moved = (
        to_plane(jnp.where(half == 0, zero, one), 0),
        to_plane(jnp.where(half == 0, one, zero), 1),
    )

    pos = vision_pos.reshape(SOURCES, PER_SOURCE)
    target = pos // SHARD
    index = jnp.arange(PER_SOURCE, dtype=jnp.int32)

    def code_of(source_half):
        source = ((x * 2 + source_half) * 4 + y) * 2 + c
        own = lax.dynamic_index_in_dim(target, source, 0, keepdims=False)
        same = (own[None, :] == own[:, None]) & (index[:, None] < index[None, :])
        rank = jnp.sum(same.astype(jnp.int32), axis=0)
        column = (own // 16) * 8 + own % 8
        to_half = (own // 8) % 2
        return ((column * 2 + to_half) * SLOTS + rank).reshape(1, PER_SOURCE)

    slot = jnp.arange(SLOTS, dtype=jnp.int32)

    def landing_of(shard_half):
        shard = ((x * 2 + shard_half) * 4 + y) * 2 + c
        hit = target == shard
        skip = jnp.sum((target < shard).astype(jnp.int32), axis=1, keepdims=True)
        rank = jnp.where(hit, index[None, :] - skip, -1)
        chosen = rank[:, None, :] == slot[None, :, None]
        local = pos - shard * SHARD + 1
        landing = jnp.sum(jnp.where(chosen, local[:, None, :], 0), axis=2) - 1
        return jnp.transpose(landing.reshape(4, 2, 8, SLOTS), (0, 2, 1, 3))

    landings = (landing_of(0), landing_of(1))

    def one_source(landing):
        return jnp.where(half == 0, landing[:, :, 0], landing[:, :, 1]).reshape(1, -1)

    def two_sources(landing):
        return jnp.where(part == 0, landing, landing[:, :, ::-1]).reshape(1, -1)

    landing = jnp.where(half == 0, landings[0], landings[1]).reshape(1, -1)

    marks = doc_ids + 1
    joined_marks = jnp.concatenate([from_behind(marks[SHARD - REACH :], 8), marks], 0)
    kdoc = lax.dynamic_slice_in_dim(joined_marks, zl * ROWS, REACH + ROWS).reshape(1, -1)
    qdoc = lax.dynamic_slice_in_dim(marks, zl * ROWS, ROWS).reshape(-1, 1)

    slots_kv = over_columns(to_slots((code_of(half),), (rows[:, QW:],)))
    blocks_kv = to_blocks([one_source(each) for each in landings], after(slots_kv, *moved))
    own_kv = merge_keys(zl_arr, landing, text, over_planes(blocks_kv))
    one_kv = from_behind(own_kv, 1)
    two_kv = from_behind(one_kv, 1)

    slots_q = to_slots((code_of(part), code_of(1 - part)), moved)
    slots_q = over_columns(after(slots_q, own_kv))
    blocks_q = to_blocks([two_sources(each) for each in landings], slots_q)
    arrived_q = over_planes(after(blocks_q, two_kv))

    out = call(
        attend_kernel, "attend", bf16(GROUPS, ROWS, QW),
        (zl_arr,), landing, qdoc, kdoc, text, two_kv, one_kv, own_kv, arrived_q,
    )
    return jnp.transpose(out, (1, 0, 2))


def solution(mesh):
    fine = Mesh(mesh.devices.reshape(SIZES), AXES)
    in_specs = (
        P(AXES, None, None),
        P(("x", "zh", "y", "c"), "zl", None),
        P(),
        P(("x", "zh", "y", "c")),
    )
    return jax.shard_map(
        body, mesh=fine, in_specs=in_specs, out_specs=P(AXES, None, None), check_vma=False
    )
```

```python
import functools

import jax
import jax.numpy as jnp
import numpy as np
from jax import lax
from jax.experimental import pallas as pl
from jax.experimental.pallas import tpu as pltpu
from jax.sharding import Mesh
from jax.sharding import PartitionSpec as P

HD = 128
QPG = 4
GROUPS = 8
QW = QPG * HD
KW = 2 * HD
PART = 2 * HD
ROWS = 128
SHARD = 1024
SLOTS = 16
SOURCES = 64
PER_SOURCE = 512
COLUMNS = 32
PLANES = 16
REACH = 256
AXES = ("x", "zh", "y", "c", "zl")
SIZES = (4, 2, 4, 2, 8)
COUNT = 512
VMEM = 48 * 1024 * 1024
PLANE_OF = (15, 1, 3, 10, 14, 9, 2, 5, 13, 7, 8, 4, 0, 11, 6, 12)
UNIT_OF = tuple(int(u) for u in np.argsort(np.array(PLANE_OF)))


def flat_id(x, zh, y, c, zl):
    return (((x * 2 + zh) * 4 + y) * 2 + c) * 8 + zl


def to_plane(value, swapped):
    ids = []
    for x in range(4):
        for y in range(4):
            for c in range(2):
                for zh in range(2):
                    for zl in range(8):
                        plane = PLANE_OF[zl * 2 + (zh ^ swapped)]
                        target = flat_id(x, plane // 8, y, c, plane % 8)
                        ids.append((flat_id(x, zh, y, c, zl), target))
    return lax.ppermute(value, AXES, ids)


def from_behind(value, steps):
    return lax.ppermute(value, AXES, [(i, i + steps) for i in range(COUNT - steps)])


def over_columns(slots):
    return lax.all_to_all(slots, ("x", "y", "c"), split_axis=0, concat_axis=0, tiled=True)


def over_planes(blocks):
    return lax.all_to_all(blocks, ("zh", "zl"), split_axis=0, concat_axis=0, tiled=True)


def after(value, *others):
    return lax.optimization_barrier((value, *others))[0]


def vmem():
    return pl.BlockSpec(memory_space=pltpu.VMEM)


def smem():
    return pl.BlockSpec(memory_space=pltpu.SMEM)


def call(kernel, name, out_shape, scalars, *arrays):
    return pl.pallas_call(
        kernel,
        out_shape=out_shape,
        in_specs=[smem()] * len(scalars) + [vmem()] * len(arrays),
        out_specs=[vmem()] * len(out_shape) if isinstance(out_shape, list) else vmem(),
        compiler_params=pltpu.CompilerParams(vmem_limit_bytes=VMEM),
        name=name,
    )(*scalars, *arrays)


def bf16(*shape):
    return jax.ShapeDtypeStruct(shape, jnp.bfloat16)


def pick(first, codes, rows):
    wanted = lax.broadcasted_iota(jnp.int32, (ROWS, codes.shape[1]), 0) + first
    onehot = jnp.where(wanted == codes, 1.0, 0.0).astype(jnp.bfloat16)
    return jnp.dot(onehot, rows, preferred_element_type=jnp.float32).astype(jnp.bfloat16)


def slots_kernel(count, *refs):
    codes, sources, out_ref = refs[:count], refs[count : 2 * count], refs[-1]
    for turn in range(count):
        for part in range(SOURCES * SLOTS // ROWS):
            picked = pick(part * ROWS, codes[turn][...], sources[turn][...])
            for i in range(ROWS // SLOTS):
                column, half = (part * (ROWS // SLOTS) + i) // 2, i % 2
                low = (half * count + turn) * SLOTS
                out_ref[column, low : low + SLOTS, :] = picked[i * SLOTS : (i + 1) * SLOTS]


def to_slots(codes, sources):
    count = len(codes)
    shape = bf16(COLUMNS, 2 * count * SLOTS, sources[0].shape[1])
    return call(functools.partial(slots_kernel, count), "to_slots", shape, (), *codes, *sources)


def blocks_kernel(low_land, high_land, slots_ref, out_ref):
    per_half, width = slots_ref.shape[1] // 2, slots_ref.shape[2]
    for half, landing in enumerate((low_land, high_land)):
        slots = slots_ref[:, half * per_half : (half + 1) * per_half, :]
        slots = slots.reshape(COLUMNS * per_half, width)
        for block in range(GROUPS):
            out_ref[half * GROUPS + block] = pick(block * ROWS, landing[...], slots)


def to_blocks(landings, slots):
    return call(blocks_kernel, "to_blocks", bf16(PLANES, ROWS, slots.shape[2]), (), *landings, slots)


def landed(first, landing):
    rows = lax.broadcasted_iota(jnp.int32, (ROWS, landing.shape[1]), 0) + first
    return jnp.max(jnp.where(rows == landing, 1.0, 0.0), axis=1, keepdims=True) > 0.0


def merge_kernel(zl_ref, landing_ref, text_ref, arrived_ref, out_ref):
    present = landed(zl_ref[0] * ROWS, landing_ref[...])
    for group in range(GROUPS):
        arrived = arrived_ref[group] + arrived_ref[GROUPS + group]
        out_ref[group] = jnp.where(present, arrived, text_ref[group, :, QW:])


def merge_keys(zl, landing, text, arrived):
    return call(merge_kernel, "merge_keys", bf16(GROUPS, ROWS, KW), (zl,), landing, text, arrived)


def prepare_kernel(
    zl_ref, landing_ref, qdoc_ref, kdoc_ref, text_ref, two_ref, one_ref, own_ref,
    query_ref, key_ref, value_ref, bias_ref,
):
    present = landed(zl_ref[0] * ROWS, landing_ref[...])
    window = REACH + ROWS
    query_pos = lax.broadcasted_iota(jnp.int32, (ROWS, window), 0) + REACH
    key_pos = lax.broadcasted_iota(jnp.int32, (ROWS, window), 1)
    allowed = (kdoc_ref[...] == qdoc_ref[...]) & (key_pos <= query_pos)
    bias_ref[...] = jnp.where(allowed, 0.0, -jnp.inf)
    for group in range(GROUPS):
        text = text_ref[group, :, :QW]
        query_ref[group] = jnp.where(present, jnp.zeros_like(text), text)
        for i, ref in enumerate((two_ref, one_ref, own_ref)):
            span = slice(i * ROWS, (i + 1) * ROWS)
            key_ref[group, :, span] = jnp.transpose(ref[group, :, :HD])
            value_ref[group, span, :] = ref[group, :, HD:]


def prepare(zl, *arrays):
    window = REACH + ROWS
    shapes = [
        bf16(GROUPS, ROWS, QW),
        bf16(GROUPS, HD, window),
        bf16(GROUPS, window, HD),
        jax.ShapeDtypeStruct((ROWS, window), jnp.float32),
    ]
    return call(prepare_kernel, "prepare", shapes, (zl,), *arrays)


def attend_kernel(query_ref, key_ref, value_ref, bias_ref, arrived_ref, out_ref):
    bias = bias_ref[...]
    factor = HD ** (-0.5)
    for group in range(GROUPS):
        queries = []
        for head in range(QPG):
            low = (head % 2) * HD
            arrived = arrived_ref[PLANE_OF[group * 2 + head // 2], :, low : low + HD]
            queries.append(arrived + query_ref[group, :, head * HD : (head + 1) * HD])
        scores = jnp.dot(
            jnp.concatenate(queries, 0), key_ref[group], preferred_element_type=jnp.float32
        )
        for head in range(QPG):
            masked = scores[head * ROWS : (head + 1) * ROWS] * factor + bias
            row_max = jnp.max(masked, axis=1, keepdims=True)
            terms = jnp.exp(masked - row_max)
            total = jnp.sum(terms, axis=1, keepdims=True)
            weights = terms.astype(jnp.bfloat16)
            summed = jnp.dot(weights, value_ref[group], preferred_element_type=jnp.float32)
            out_ref[group, :, head * HD : (head + 1) * HD] = (summed / total).astype(jnp.bfloat16)


def body(text_rows, vision_rows, vision_pos, doc_ids):
    rows = vision_rows.reshape(PER_SOURCE, QW + KW)
    x, half, y, c, zl = [lax.axis_index(axis) for axis in AXES]
    zl_arr = zl.reshape(1)
    part = jnp.asarray(UNIT_OF, jnp.int32)[half * 8 + zl] % 2
    text = jnp.transpose(text_rows, (1, 0, 2))

    zero, one = rows[:, :PART], rows[:, PART:QW]
    moved = (
        to_plane(jnp.where(half == 0, zero, one), 0),
        to_plane(jnp.where(half == 0, one, zero), 1),
    )

    pos = vision_pos.reshape(SOURCES, PER_SOURCE)
    target = pos // SHARD
    index = jnp.arange(PER_SOURCE, dtype=jnp.int32)

    def code_of(source_half):
        source = ((x * 2 + source_half) * 4 + y) * 2 + c
        own = lax.dynamic_index_in_dim(target, source, 0, keepdims=False)
        same = (own[None, :] == own[:, None]) & (index[:, None] < index[None, :])
        rank = jnp.sum(same.astype(jnp.int32), axis=0)
        column = (own // 16) * 8 + own % 8
        to_half = (own // 8) % 2
        return ((column * 2 + to_half) * SLOTS + rank).reshape(1, PER_SOURCE)

    slot = jnp.arange(SLOTS, dtype=jnp.int32)

    def landing_of(shard_half):
        shard = ((x * 2 + shard_half) * 4 + y) * 2 + c
        hit = target == shard
        skip = jnp.sum((target < shard).astype(jnp.int32), axis=1, keepdims=True)
        rank = jnp.where(hit, index[None, :] - skip, -1)
        chosen = rank[:, None, :] == slot[None, :, None]
        local = pos - shard * SHARD + 1
        landing = jnp.sum(jnp.where(chosen, local[:, None, :], 0), axis=2) - 1
        return jnp.transpose(landing.reshape(4, 2, 8, SLOTS), (0, 2, 1, 3))

    landings = (landing_of(0), landing_of(1))

    def one_source(landing):
        return jnp.where(half == 0, landing[:, :, 0], landing[:, :, 1]).reshape(1, -1)

    def two_sources(landing):
        return jnp.where(part == 0, landing, landing[:, :, ::-1]).reshape(1, -1)

    landing = jnp.where(half == 0, landings[0], landings[1]).reshape(1, -1)

    marks = doc_ids + 1
    joined_marks = jnp.concatenate([from_behind(marks[SHARD - REACH :], 8), marks], 0)
    kdoc = lax.dynamic_slice_in_dim(joined_marks, zl * ROWS, REACH + ROWS).reshape(1, -1)
    qdoc = lax.dynamic_slice_in_dim(marks, zl * ROWS, ROWS).reshape(-1, 1)

    slots_kv = over_columns(to_slots((code_of(half),), (rows[:, QW:],)))
    blocks_kv = to_blocks([one_source(each) for each in landings], after(slots_kv, *moved))
    own_kv = merge_keys(zl_arr, landing, text, over_planes(blocks_kv))
    one_kv = from_behind(own_kv, 1)
    two_kv = from_behind(one_kv, 1)

    slots_q = to_slots((code_of(part), code_of(1 - part)), moved)
    slots_q = over_columns(after(slots_q, own_kv))
    blocks_q = to_blocks([two_sources(each) for each in landings], slots_q)
    arrived_q = over_planes(after(blocks_q, two_kv))

    ready = prepare(zl_arr, landing, qdoc, kdoc, text, two_kv, one_kv, own_kv)
    out = call(attend_kernel, "attend", bf16(GROUPS, ROWS, QW), (), *ready, arrived_q)
    return jnp.transpose(out, (1, 0, 2))


def solution(mesh):
    fine = Mesh(mesh.devices.reshape(SIZES), AXES)
    in_specs = (
        P(AXES, None, None),
        P(("x", "zh", "y", "c"), "zl", None),
        P(),
        P(("x", "zh", "y", "c")),
    )
    return jax.shard_map(
        body, mesh=fine, in_specs=in_specs, out_specs=P(AXES, None, None), check_vma=False
    )
```

```python
import functools

import jax
import jax.numpy as jnp
import numpy as np
from jax import lax
from jax.experimental import pallas as pl
from jax.experimental.pallas import tpu as pltpu
from jax.sharding import Mesh
from jax.sharding import PartitionSpec as P

HD = 128
QPG = 4
GROUPS = 8
QW = QPG * HD
KW = 2 * HD
PART = 2 * HD
ROWS = 128
SHARD = 1024
SLOTS = 16
SOURCES = 64
PER_SOURCE = 512
COLUMNS = 32
PLANES = 16
REACH = 256
AXES = ("x", "zh", "y", "c", "zl")
SIZES = (4, 2, 4, 2, 8)
COUNT = 512
VMEM = 48 * 1024 * 1024
PLANE_OF = (15, 1, 3, 10, 14, 9, 2, 5, 13, 7, 8, 4, 0, 11, 6, 12)
UNIT_OF = tuple(int(u) for u in np.argsort(np.array(PLANE_OF)))


def flat_id(x, zh, y, c, zl):
    return (((x * 2 + zh) * 4 + y) * 2 + c) * 8 + zl


def to_plane(value, swapped):
    ids = []
    for x in range(4):
        for y in range(4):
            for c in range(2):
                for zh in range(2):
                    for zl in range(8):
                        plane = PLANE_OF[zl * 2 + (zh ^ swapped)]
                        target = flat_id(x, plane // 8, y, c, plane % 8)
                        ids.append((flat_id(x, zh, y, c, zl), target))
    return lax.ppermute(value, AXES, ids)


def from_behind(value, steps):
    return lax.ppermute(value, AXES, [(i, i + steps) for i in range(COUNT - steps)])


def over_columns(slots):
    return lax.all_to_all(slots, ("x", "y", "c"), split_axis=0, concat_axis=0, tiled=True)


def over_planes(blocks):
    return lax.all_to_all(blocks, ("zh", "zl"), split_axis=0, concat_axis=0, tiled=True)


def after(value, *others):
    return lax.optimization_barrier((value, *others))[0]


def vmem():
    return pl.BlockSpec(memory_space=pltpu.VMEM)


def smem():
    return pl.BlockSpec(memory_space=pltpu.SMEM)


def call(kernel, name, out_shape, scalars, *arrays):
    return pl.pallas_call(
        kernel,
        out_shape=out_shape,
        in_specs=[smem()] * len(scalars) + [vmem()] * len(arrays),
        out_specs=vmem(),
        compiler_params=pltpu.CompilerParams(vmem_limit_bytes=VMEM),
        name=name,
    )(*scalars, *arrays)


def bf16(*shape):
    return jax.ShapeDtypeStruct(shape, jnp.bfloat16)


def pick(first, codes, rows):
    wanted = lax.broadcasted_iota(jnp.int32, (ROWS, codes.shape[1]), 0) + first
    onehot = jnp.where(wanted == codes, 1.0, 0.0).astype(jnp.bfloat16)
    return jnp.dot(onehot, rows, preferred_element_type=jnp.float32).astype(jnp.bfloat16)


def slots_kernel(count, *refs):
    codes, sources, out_ref = refs[:count], refs[count : 2 * count], refs[-1]
    for turn in range(count):
        for part in range(SOURCES * SLOTS // ROWS):
            picked = pick(part * ROWS, codes[turn][...], sources[turn][...])
            for i in range(ROWS // SLOTS):
                column, half = (part * (ROWS // SLOTS) + i) // 2, i % 2
                low = (half * count + turn) * SLOTS
                out_ref[column, low : low + SLOTS, :] = picked[i * SLOTS : (i + 1) * SLOTS]


def to_slots(codes, sources):
    count = len(codes)
    shape = bf16(COLUMNS, 2 * count * SLOTS, sources[0].shape[1])
    return call(functools.partial(slots_kernel, count), "to_slots", shape, (), *codes, *sources)


def blocks_kernel(low_land, high_land, slots_ref, out_ref):
    per_half, width = slots_ref.shape[1] // 2, slots_ref.shape[2]
    for half, landing in enumerate((low_land, high_land)):
        slots = slots_ref[:, half * per_half : (half + 1) * per_half, :]
        slots = slots.reshape(COLUMNS * per_half, width)
        for block in range(GROUPS):
            out_ref[half * GROUPS + block] = pick(block * ROWS, landing[...], slots)


def to_blocks(landings, slots):
    return call(blocks_kernel, "to_blocks", bf16(PLANES, ROWS, slots.shape[2]), (), *landings, slots)


def landed(first, landing):
    rows = lax.broadcasted_iota(jnp.int32, (ROWS, landing.shape[1]), 0) + first
    return jnp.max(jnp.where(rows == landing, 1.0, 0.0), axis=1, keepdims=True) > 0.0


def merge_kernel(zl_ref, landing_ref, text_ref, arrived_ref, out_ref):
    present = landed(zl_ref[0] * ROWS, landing_ref[...])
    for group in range(GROUPS):
        arrived = arrived_ref[group] + arrived_ref[GROUPS + group]
        out_ref[group] = jnp.where(present, arrived, text_ref[group, :, QW:])


def merge_keys(zl, landing, text, arrived):
    return call(merge_kernel, "merge_keys", bf16(GROUPS, ROWS, KW), (zl,), landing, text, arrived)


def attend_kernel(zl_ref, landing_ref, qdoc_ref, kdoc_ref, text_ref, two_ref, one_ref, own_ref, arrived_ref, out_ref):
    present = landed(zl_ref[0] * ROWS, landing_ref[...])
    row = lax.broadcasted_iota(jnp.int32, (ROWS, ROWS), 0)
    lower = lax.broadcasted_iota(jnp.int32, (ROWS, ROWS), 1) <= row
    qdoc, kdoc = qdoc_ref[...], kdoc_ref[...]
    fold_ok = jnp.where(lower, kdoc[:, REACH:], kdoc[:, :ROWS]) == qdoc
    one_ok = kdoc[:, ROWS:REACH] == qdoc
    factor = HD ** (-0.5)
    for group in range(GROUPS):
        joined = jnp.concatenate([two_ref[group], one_ref[group], own_ref[group]], 0)
        keys, values = joined[:, :HD], joined[:, HD:]
        queries = []
        for head in range(QPG):
            low = (head % 2) * HD
            arrived = arrived_ref[PLANE_OF[group * 2 + head // 2], :, low : low + HD]
            text = text_ref[group, :, head * HD : (head + 1) * HD]
            queries.append(jnp.where(present, arrived, text))
        scores = lax.dot_general(
            jnp.concatenate(queries, 0),
            keys,
            (((1,), (1,)), ((), ())),
            preferred_element_type=jnp.float32,
        )
        for head in range(QPG):
            block = scores[head * ROWS : (head + 1) * ROWS]
            fold = jnp.where(lower, block[:, REACH:], block[:, :ROWS]) * factor
            fold = jnp.where(fold_ok, fold, -jnp.inf)
            one = jnp.where(one_ok, block[:, ROWS:REACH] * factor, -jnp.inf)
            row_max = jnp.max(jnp.maximum(fold, one), axis=1, keepdims=True)
            fold, one = jnp.exp(fold - row_max), jnp.exp(one - row_max)
            total = jnp.sum(fold + one, axis=1, keepdims=True)
            terms = [jnp.where(lower, 0.0, fold), one, jnp.where(lower, fold, 0.0)]
            weights = jnp.concatenate(terms, 1).astype(jnp.bfloat16)
            summed = jnp.dot(weights, values, preferred_element_type=jnp.float32)
            out_ref[group, :, head * HD : (head + 1) * HD] = (summed / total).astype(jnp.bfloat16)


def body(text_rows, vision_rows, vision_pos, doc_ids):
    rows = vision_rows.reshape(PER_SOURCE, QW + KW)
    x, half, y, c, zl = [lax.axis_index(axis) for axis in AXES]
    zl_arr = zl.reshape(1)
    part = jnp.asarray(UNIT_OF, jnp.int32)[half * 8 + zl] % 2
    text = jnp.transpose(text_rows, (1, 0, 2))

    zero, one = rows[:, :PART], rows[:, PART:QW]
    moved = (
        to_plane(jnp.where(half == 0, zero, one), 0),
        to_plane(jnp.where(half == 0, one, zero), 1),
    )

    pos = vision_pos.reshape(SOURCES, PER_SOURCE)
    target = pos // SHARD
    index = jnp.arange(PER_SOURCE, dtype=jnp.int32)

    def code_of(source_half):
        source = ((x * 2 + source_half) * 4 + y) * 2 + c
        own = lax.dynamic_index_in_dim(target, source, 0, keepdims=False)
        same = (own[None, :] == own[:, None]) & (index[:, None] < index[None, :])
        rank = jnp.sum(same.astype(jnp.int32), axis=0)
        column = (own // 16) * 8 + own % 8
        to_half = (own // 8) % 2
        return ((column * 2 + to_half) * SLOTS + rank).reshape(1, PER_SOURCE)

    slot = jnp.arange(SLOTS, dtype=jnp.int32)

    def landing_of(shard_half):
        shard = ((x * 2 + shard_half) * 4 + y) * 2 + c
        hit = target == shard
        skip = jnp.sum((target < shard).astype(jnp.int32), axis=1, keepdims=True)
        rank = jnp.where(hit, index[None, :] - skip, -1)
        chosen = rank[:, None, :] == slot[None, :, None]
        local = pos - shard * SHARD + 1
        landing = jnp.sum(jnp.where(chosen, local[:, None, :], 0), axis=2) - 1
        return jnp.transpose(landing.reshape(4, 2, 8, SLOTS), (0, 2, 1, 3))

    landings = (landing_of(0), landing_of(1))

    def one_source(landing):
        return jnp.where(half == 0, landing[:, :, 0], landing[:, :, 1]).reshape(1, -1)

    def two_sources(landing):
        return jnp.where(part == 0, landing, landing[:, :, ::-1]).reshape(1, -1)

    landing = jnp.where(half == 0, landings[0], landings[1]).reshape(1, -1)

    marks = doc_ids + 1
    joined_marks = jnp.concatenate([from_behind(marks[SHARD - REACH :], 8), marks], 0)
    kdoc = lax.dynamic_slice_in_dim(joined_marks, zl * ROWS, REACH + ROWS).reshape(1, -1)
    qdoc = lax.dynamic_slice_in_dim(marks, zl * ROWS, ROWS).reshape(-1, 1)

    slots_kv = over_columns(to_slots((code_of(half),), (rows[:, QW:],)))
    blocks_kv = to_blocks([one_source(each) for each in landings], after(slots_kv, *moved))
    own_kv = merge_keys(zl_arr, landing, text, over_planes(blocks_kv))
    one_kv = from_behind(own_kv, 1)
    two_kv = from_behind(one_kv, 1)

    slots_q = to_slots((code_of(part), code_of(1 - part)), moved)
    slots_q = over_columns(after(slots_q, own_kv))
    blocks_q = to_blocks([two_sources(each) for each in landings], slots_q)
    arrived_q = over_planes(after(blocks_q, two_kv))

    out = call(
        attend_kernel, "attend", bf16(GROUPS, ROWS, QW),
        (zl_arr,), landing, qdoc, kdoc, text, two_kv, one_kv, own_kv, arrived_q,
    )
    return jnp.transpose(out, (1, 0, 2))


def solution(mesh):
    fine = Mesh(mesh.devices.reshape(SIZES), AXES)
    in_specs = (
        P(AXES, None, None),
        P(("x", "zh", "y", "c"), "zl", None),
        P(),
        P(("x", "zh", "y", "c")),
    )
    return jax.shard_map(
        body, mesh=fine, in_specs=in_specs, out_specs=P(AXES, None, None), check_vma=False
    )
```
